512 devices in a mesh: row: 16 (over x, y), col: 32 (over z, core).
Axes of the slice: x: 4, y: 4, z: 16, core: 2. Of those that a mesh axis runs over, the one named last changes fastest.
Arguments:
- integrals: bfloat16 [512, 16, 6, 128, 128], P(('col', 'row')), may hold values from -0.21875 to 0.21875
- green_panel: bfloat16 [480, 2048], P('col'), may hold values from -6 to 6
- neighbours: int32 [16, 6], replicated, may hold values from 0 to 15, as said below
- slot_counts: int32 [16], replicated, may hold values from 1 to 6, as said below
Outputs:
- contracted: bfloat16 [512, 2048, 480], P('col', 'row')
The draws below stay inside these ranges and needn't reach their ends.
Inputs may be any that keep to these rules, and one draw needn't show every extreme that they name: `neighbours`: atom indices. `slot_counts`: some atom uses all 6 slots.
All inputs are finite; a program needn't handle non-finite values.
Results may differ from the reference program's by a relative error of at most 0.001.
Values may be sent and summed in bfloat16 or wider, within the bound.
A program may use at most 64 MiB of HBM per device.

```python
import jax
import jax.numpy as jnp
from jax import lax

BS = 128
KMAX = 6
NATOM = 16
NORB = 2048
NAUX = 512
NOCC = 480


def draw_neighbours(key, part):
    key = jax.random.fold_in(key, 11)
    return jax.random.randint(key, (NATOM, KMAX), 0, NATOM).astype(jnp.int32)


def draw_slot_counts(key, part):
    key = jax.random.fold_in(key, 23)
    first_key, second_key = jax.random.split(key)
    values = jax.random.randint(first_key, (NATOM,), 1, KMAX + 1).astype(jnp.int32)
    picked = jax.random.randint(second_key, (), 0, NATOM)
    return values.at[picked].set(KMAX).astype(jnp.int32)


def steps_of(stream_key, dims, shards, least, largest):
    gain = 1.0
    for axis_at, parts in shards:
        steps = jax.random.uniform(jax.random.fold_in(jax.random.fold_in(stream_key, 6), axis_at), (parts,), jnp.float32, least / len(shards), largest / len(shards))
        gain = gain * jnp.repeat(jnp.exp(steps), dims[axis_at] // parts).reshape((-1,) + (1,) * (len(dims) - 1 - axis_at))
    return gain


def centred(key, extent, scale, bound, pieces=(), kind=jnp.bfloat16):
    factor_of = steps_of(key, extent, pieces, -0.22, 0.18) if pieces else 1.0
    drawn = jax.random.normal(key, extent, jnp.float32) * scale * factor_of
    return jnp.minimum(jnp.maximum(drawn, -bound), bound).astype(kind)


def setup_inputs(seed: int = 0) -> dict:
    seeds = jax.random.split(jax.random.key(seed), 5)
    return {
        "integrals": centred(seeds[0], (NAUX, NATOM, KMAX, BS, BS), (KMAX * BS) ** -0.5, 0.21875, ((0, 512),)),
        "green_panel": centred(seeds[1], (NOCC, NORB), 1.0, 6.0, ((0, 32),)),
        "neighbours": draw_neighbours(jax.random.fold_in(seeds[4], 71), 0),
        "slot_counts": draw_slot_counts(jax.random.fold_in(seeds[4], 71), 0),
    }


def reference(integrals, green_panel, neighbours, slot_counts):
    keep_mask = jnp.arange(KMAX, dtype=jnp.int32)[None, :] < slot_counts[:, None]
    spread = green_panel.reshape(NOCC, NATOM, BS)
    chosen = jnp.take(spread, neighbours.reshape(-1), axis=1).reshape(NOCC, NATOM, KMAX, BS)
    chosen = jnp.where(keep_mask[None, :, :, None], chosen, jnp.zeros((), chosen.dtype)).astype(jnp.float32)

    def per_aux(aux_block):
        product = jnp.einsum('akmn,iakn->ami', aux_block.astype(jnp.float32), chosen)
        return product.reshape(NORB, NOCC).astype(jnp.bfloat16)

    return lax.map(per_aux, integrals)
```

```python
import jax
import jax.numpy as jnp
from jax import lax
from jax.sharding import PartitionSpec as P


def per_device(integrals, green_panel, neighbours, slot_counts):
    atom_count = neighbours.shape[0]
    slot_count = neighbours.shape[1]
    block_width = integrals.shape[-1]
    keep = jnp.arange(slot_count, dtype=jnp.int32)[None, :] < slot_counts[:, None]
    green = lax.all_gather(green_panel, "col", axis=0, tiled=True)
    rows = green.shape[0]
    spread = green.reshape(rows, atom_count, block_width)
    chosen = jnp.take(spread, neighbours.reshape(-1), axis=1)
    chosen = chosen.reshape(rows, atom_count, slot_count, block_width)
    chosen = jnp.where(keep[None, :, :, None], chosen, jnp.zeros((), chosen.dtype))
    local = integrals[0]
    out = jnp.einsum(
        "akmn,iakn->ami", local, chosen, preferred_element_type=jnp.float32
    ).astype(jnp.bfloat16)
    out = lax.all_to_all(out, "row", split_axis=0, concat_axis=0, tiled=True)
    return out


def solution(mesh):
    return jax.shard_map(
        per_device,
        mesh=mesh,
        in_specs=(P(("col", "row"), None, None, None, None), P("col", None), P(), P()),
        out_specs=P("col", "row", None),
        check_vma=False,
    )
```

```python
import functools

import jax
import jax.numpy as jnp
from jax import lax
from jax.experimental import pallas as pl
from jax.experimental.pallas import tpu as pltpu
from jax.sharding import PartitionSpec as P

MESH = pl.DeviceIdType.MESH
SIDE = 4
DEPTH = 16
FAR = DEPTH // 2
ATOMS = 16
SLOTS = 6
BS = 128
PANEL = 15
SHARD = 16
NOCC = 480
WIDE = SLOTS * BS
PARTS = 2
CHUNKS = 2
HALF = BS // 2
ROWS = HALF // CHUNKS
NU = ATOMS // PARTS


def kernel(
    ints, panel, nbr, cnt, out,
    g0, g1, g2, g3, g4, g5, g6, g7, g8,
    rows, mid, fin, w32, obuf,
    ring_s, ring_r, sib_s, sib_r, one_s, one_r, two_s, two_r, local, osem,
):
    green = [g0, g1, g2, g3, g4, g5, g6, g7, g8]
    row = lax.axis_index("row")
    col = lax.axis_index("col")
    x, y = row // SIDE, row % SIDE
    z, core = col // 2, col % 2

    def at(dx=0, dy=0, dz=0, dc=0):
        return (
            ((x + dx) % SIDE) * SIDE + (y + dy) % SIDE,
            ((z + dz + DEPTH) % DEPTH) * 2 + (core + dc) % 2,
        )

    partners = [at(dx=d) for d in (1, 2, 3)] + [at(dy=d) for d in (1, 2, 3)]
    partners += [at(dz=1), at(dz=-1), at(dc=1)]
    barrier = pltpu.get_barrier_semaphore()
    for p in partners:
        pl.semaphore_signal(barrier, inc=1, device_id=p, device_id_type=MESH)

    load = pltpu.make_async_copy(panel, rows, local.at[0])
    load.start()
    span = [pl.ds(h * HALF + c * ROWS, ROWS) for h in range(2) for c in range(CHUNKS)]

    def source(h, c, d):
        m = span[h * CHUNKS + c]
        if h == 0:
            return ints.at[(x + d) % SIDE, :, :, m, :]
        return ints.at[:, (y + d) % SIDE, :, m, :]

    own = []
    for h in range(2):
        for c in range(CHUNKS):
            cp = pltpu.make_async_copy(
                source(h, c, 0), mid.at[h, c, 0], local.at[1 + h * CHUNKS + c]
            )
            cp.start()
            own.append(cp)
    load.wait()
    for nu in range(ATOMS):
        g0[nu, pl.ds(0, SHARD), :] = jnp.concatenate(
            [rows[:, nu * BS : (nu + 1) * BS], jnp.zeros((1, BS), jnp.bfloat16)], axis=0
        )
    w32[...] = jnp.zeros_like(w32)
    pl.semaphore_wait(barrier, len(partners))

    def nus(p):
        return pl.ds(p * NU, NU)

    def ring(d, q, p):
        q_src = 0 if d == 0 else q
        q_dst = 0 if d + 1 == FAR else q
        return pltpu.make_async_remote_copy(
            src_ref=green[d].at[nus(p), pl.ds(q_src * SHARD, SHARD), :],
            dst_ref=green[d + 1].at[nus(p), pl.ds(q_dst * SHARD, SHARD), :],
            send_sem=ring_s.at[d, q, p],
            recv_sem=ring_r.at[d, q, p],
            device_id=at(dz=1 if q == 0 else -1),
            device_id_type=MESH,
        )

    def moves(d, q, p):
        return d + 1 < FAR or q == p

    def shared(d):
        return 1 if d in (0, FAR) else 2

    def sib(d, q):
        n = shared(d)
        return pltpu.make_async_remote_copy(
            src_ref=green[d].at[:, pl.ds(q * SHARD, SHARD), :],
            dst_ref=green[d].at[:, pl.ds((q + n) * SHARD, SHARD), :],
            send_sem=sib_s.at[d, q],
            recv_sem=sib_r.at[d, q],
            device_id=at(dc=1),
            device_id_type=MESH,
        )

    def first(h, c, d):
        return pltpu.make_async_remote_copy(
            src_ref=source(h, c, d),
            dst_ref=mid.at[h, c, d],
            send_sem=one_s.at[h, c, d],
            recv_sem=one_r.at[h, c, d],
            device_id=at(dx=d) if h == 0 else at(dy=d),
            device_id_type=MESH,
        )

    def held(h, c, e):
        return mid.at[h, c, :, (y + e) % SIDE if h == 0 else (x + e) % SIDE]

    def second(h, c, e):
        return pltpu.make_async_remote_copy(
            src_ref=held(h, c, e),
            dst_ref=fin.at[h, c, e],
            send_sem=two_s.at[h, c, e],
            recv_sem=two_r.at[h, c, e],
            device_id=at(dy=e) if h == 0 else at(dx=e),
            device_id_type=MESH,
        )

    def keep(h, c):
        return pltpu.make_async_copy(
            held(h, c, 0), fin.at[h, c, 0], local.at[1 + (2 + h) * CHUNKS + c]
        )

    def ring_step(d):
        for p in range(PARTS):
            for q in range(2):
                if moves(d - 1, q, p):
                    ring(d - 1, q, p).wait_recv()
                    if d < FAR and moves(d, q, p):
                        ring(d, q, p).start()
        for q in range(shared(d)):
            sib(d, q).start()

    def forward(c):
        for h in range(2):
            own[h * CHUNKS + c].wait()
            for d in (1, 3, 2):
                first(h, c, d).wait_recv()
            for e in (1, 3, 2):
                second(h, c, e).start()
            keep(h, c).start()

    def weigh(d):
        n = shared(d)
        for q in range(n):
            sib(d, q).wait_recv()
        lanes = 2 * n * SHARD
        at_row = lax.broadcasted_iota(jnp.int32, (NOCC, lanes), 0)
        lane = lax.broadcasted_iota(jnp.int32, (NOCC, lanes), 1)
        q, j = lane // SHARD, lane % SHARD
        if n == 2:
            from_z = jnp.where(q % 2 == 0, z - d + DEPTH, z + d) % DEPTH
        else:
            from_z = (z + d) % DEPTH
        from_core = jnp.where(q < n, core, 1 - core)
        to = (from_z * 2 + from_core) * PANEL + j
        place = ((to == at_row) & (j < PANEL)).astype(jnp.float32).astype(jnp.bfloat16)
        parts = []
        for k in range(SLOTS):
            g = green[d][nbr[row, k], pl.ds(0, lanes), :]
            parts.append(jnp.where(k < cnt[row], g, jnp.zeros_like(g)))
        w32[...] += jnp.dot(
            place, jnp.concatenate(parts, axis=1), preferred_element_type=jnp.float32
        )

    def contract(c):
        for h in range(2):
            keep(h, c).wait()
            for e in (1, 3, 2):
                second(h, c, e).wait_recv()
            blocks = [
                fin[h, c, :, :, k].reshape(SIDE * SIDE * ROWS, BS) for k in range(SLOTS)
            ]
            lhs = jnp.concatenate(blocks, axis=1)
            res = lax.dot_general(
                lhs, w32[...].astype(jnp.bfloat16), (((1,), (1,)), ((), ())),
                preferred_element_type=jnp.float32,
            ).astype(jnp.bfloat16)
            res = res.reshape(SIDE, SIDE, ROWS, NOCC)
            for e in range(SIDE):
                for d in range(SIDE):
                    dx, dy = (d, e) if h == 0 else (e, d)
                    p = ((x - dx + SIDE) % SIDE) * SIDE + (y - dy + SIDE) % SIDE
                    obuf[p, span[h * CHUNKS + c], :] = res[e, d]

    for p in range(PARTS):
        for q in range(2):
            ring(0, q, p).start()
    sib(0, 0).start()
    for c in range(CHUNKS):
        for d in (1, 3, 2):
            for h in range(2):
                first(h, c, d).start()

    ring_step(1)
    weigh(0)
    ring_step(2)
    weigh(1)
    ring_step(3)
    weigh(2)
    forward(0)
    ring_step(4)
    weigh(3)
    ring_step(5)
    weigh(4)
    forward(1)
    ring_step(6)
    weigh(5)
    ring_step(7)
    weigh(6)
    ring_step(8)
    weigh(7)
    weigh(8)
    contract(0)
    contract(1)
    store = pltpu.make_async_copy(obuf, out, osem)
    store.start()

    for d in range(FAR):
        for q in range(2):
            for p in range(PARTS):
                if moves(d, q, p):
                    ring(d, q, p).wait_send()
    for d in range(FAR + 1):
        for q in range(shared(d)):
            sib(d, q).wait_send()
    for h in range(2):
        for c in range(CHUNKS):
            for d in (1, 3, 2):
                first(h, c, d).wait_send()
                second(h, c, d).wait_send()
    store.wait()


def per_device(integrals, green_panel, neighbours, slot_counts):
    blocks = integrals.reshape(SIDE, SIDE, SLOTS, BS, BS)
    hbm = pl.BlockSpec(memory_space=pl.ANY)
    smem = pl.BlockSpec(memory_space=pltpu.SMEM)
    bf16, f32 = jnp.bfloat16, jnp.float32
    dma = pltpu.SemaphoreType.DMA
    return pl.pallas_call(
        kernel,
        out_shape=jax.ShapeDtypeStruct((ATOMS, BS, NOCC), bf16),
        in_specs=[hbm, hbm, smem, smem],
        out_specs=hbm,
        scratch_shapes=[pltpu.VMEM((ATOMS, 4 * SHARD, BS), bf16)] * (FAR + 1)
        + [
            pltpu.VMEM((PANEL, ATOMS * BS), bf16),
            pltpu.VMEM((2, CHUNKS, SIDE, SIDE, SLOTS, ROWS, BS), bf16),
            pltpu.VMEM((2, CHUNKS, SIDE, SIDE, SLOTS, ROWS, BS), bf16),
            pltpu.VMEM((NOCC, WIDE), f32),
            pltpu.VMEM((ATOMS, BS, NOCC), bf16),
            dma((FAR, 2, PARTS)),
            dma((FAR, 2, PARTS)),
            dma((FAR + 1, 2)),
            dma((FAR + 1, 2)),
            dma((2, CHUNKS, SIDE)),
            dma((2, CHUNKS, SIDE)),
            dma((2, CHUNKS, SIDE)),
            dma((2, CHUNKS, SIDE)),
            dma((1 + 4 * CHUNKS,)),
            dma,
        ],
        compiler_params=pltpu.CompilerParams(
            collective_id=0, has_side_effects=True, vmem_limit_bytes=56 << 20
        ),
    )(blocks, green_panel, neighbours, slot_counts)


def solution(mesh):
    return jax.shard_map(
        per_device,
        mesh=mesh,
        in_specs=(P(("col", "row"), None, None, None, None), P("col", None), P(), P()),
        out_specs=P("col", "row", None),
        check_vma=False,
    )
```

```python
import functools

import jax
import jax.numpy as jnp
from jax import lax
from jax.experimental import pallas as pl
from jax.experimental.pallas import tpu as pltpu
from jax.sharding import PartitionSpec as P

MESH = pl.DeviceIdType.MESH
SIDE = 4
DEPTH = 16
FAR = DEPTH // 2
ATOMS = 16
SLOTS = 6
BS = 128
PANEL = 15
SHARD = 16
NOCC = 480
WIDE = SLOTS * BS
PARTS = 2
HALF = SLOTS // 2
CHUNKS = HALF
NU = ATOMS // PARTS
GROUP = 4


def exchange(
    ints, panel, nbr_in, cnt_in, fin, wout,
    g0, g1, g2, g3, g4, g5, g6, g7, g8,
    nbr, cnt, rows, mid, w32, w16,
    ready, ring_s, ring_r, sib_s, sib_r, one_s, one_r, two_s, two_r, local,
):
    green = [g0, g1, g2, g3, g4, g5, g6, g7, g8]
    row = lax.axis_index("row")
    col = lax.axis_index("col")
    x, y = row // SIDE, row % SIDE
    z, core = col // 2, col % 2

    def at(dx=0, dy=0, dz=0, dc=0):
        return (
            ((x + dx) % SIDE) * SIDE + (y + dy) % SIDE,
            ((z + dz + DEPTH) % DEPTH) * 2 + (core + dc) % 2,
        )

    up_first = z >= FAR + 1
    down_first = (z >= 1) & (z <= FAR + 1)
    partners = [at(dx=d) for d in (1, 2, 3)] + [at(dy=d) for d in (1, 2, 3)] + [at(dc=1)]
    barrier = pltpu.get_barrier_semaphore()
    for p in partners:
        pl.semaphore_signal(barrier, inc=1, device_id=p, device_id_type=MESH)

    @pl.when(jnp.logical_not(up_first))
    def _():
        pl.semaphore_signal(barrier, inc=1, device_id=at(dz=1), device_id_type=MESH)

    @pl.when(jnp.logical_not(down_first))
    def _():
        pl.semaphore_signal(barrier, inc=1, device_id=at(dz=-1), device_id_type=MESH)

    load = pltpu.make_async_copy(panel, rows, local.at[0])
    load.start()
    tables = [
        pltpu.make_async_copy(nbr_in, nbr, local.at[1 + 4 * CHUNKS]),
        pltpu.make_async_copy(cnt_in, cnt, local.at[2 + 4 * CHUNKS]),
    ]
    for cp in tables:
        cp.start()

    def source(h, c, d):
        if h == 0:
            return ints.at[(x + d) % SIDE, :, c]
        return ints.at[:, (y + d) % SIDE, HALF + c]

    def landing(h, c):
        return mid.at[h, c, x if h == 0 else y]

    own = []
    for c in range(CHUNKS):
        for h in range(2):
            cp = pltpu.make_async_copy(
                source(h, c, 0), landing(h, c), local.at[1 + h * CHUNKS + c]
            )
            cp.start()
            own.append(cp)
    load.wait()
    for nu in range(ATOMS):
        g0[nu, pl.ds(0, SHARD), :] = jnp.concatenate(
            [rows[:, nu * BS : (nu + 1) * BS], jnp.zeros((1, BS), jnp.bfloat16)], axis=0
        )
    w32[...] = jnp.zeros_like(w32)
    expected = len(partners) + up_first.astype(jnp.int32) + down_first.astype(jnp.int32)
    pl.semaphore_wait(barrier, expected)

    @pl.when(up_first)
    def _():
        pl.semaphore_signal(ready.at[0], inc=1, device_id=at(dz=1), device_id_type=MESH)

    @pl.when(down_first)
    def _():
        pl.semaphore_signal(ready.at[1], inc=1, device_id=at(dz=-1), device_id_type=MESH)

    def nus(p):
        return pl.ds(p * NU, NU)

    def ring(d, q, p):
        q_src = 0 if d == 0 else q
        q_dst = 0 if d + 1 == FAR else q
        return pltpu.make_async_remote_copy(
            src_ref=green[d].at[nus(p), pl.ds(q_src * SHARD, SHARD), :],
            dst_ref=green[d + 1].at[nus(p), pl.ds(q_dst * SHARD, SHARD), :],
            send_sem=ring_s.at[d, q, p],
            recv_sem=ring_r.at[d, q, p],
            device_id=at(dz=1 if q == 0 else -1),
            device_id_type=MESH,
        )

    def moves(d, q, p):
        return d + 1 < FAR or q == p

    def shared(d):
        return 1 if d in (0, FAR) else 2

    def sib(d, q):
        n = shared(d)
        return pltpu.make_async_remote_copy(
            src_ref=green[d].at[:, pl.ds(q * SHARD, SHARD), :],
            dst_ref=green[d].at[:, pl.ds((q + n) * SHARD, SHARD), :],
            send_sem=sib_s.at[d, q],
            recv_sem=sib_r.at[d, q],
            device_id=at(dc=1),
            device_id_type=MESH,
        )

    def first(h, c, d):
        return pltpu.make_async_remote_copy(
            src_ref=source(h, c, d),
            dst_ref=landing(h, c),
            send_sem=one_s.at[h, c, d],
            recv_sem=one_r.at[h, c, d],
            device_id=at(dx=d) if h == 0 else at(dy=d),
            device_id_type=MESH,
        )

    def held(h, c, e):
        return mid.at[h, c, :, (y + e) % SIDE if h == 0 else (x + e) % SIDE]

    def final(h, c):
        return fin.at[:, y, c] if h == 0 else fin.at[x, :, HALF + c]

    def second(h, c, e):
        return pltpu.make_async_remote_copy(
            src_ref=held(h, c, e),
            dst_ref=final(h, c),
            send_sem=two_s.at[h, c, e],
            recv_sem=two_r.at[h, c, e],
            device_id=at(dy=e) if h == 0 else at(dx=e),
            device_id_type=MESH,
        )

    def keep(h, c):
        return pltpu.make_async_copy(
            held(h, c, 0), final(h, c), local.at[1 + (2 + h) * CHUNKS + c]
        )

    def ring_step(d):
        for p in range(PARTS):
            for q in range(2):
                if moves(d - 1, q, p):
                    ring(d - 1, q, p).wait_recv()
                    if d < FAR and moves(d, q, p):
                        ring(d, q, p).start()
        for q in range(shared(d)):
            sib(d, q).start()

    def forward(c):
        for h in range(2):
            own[c * 2 + h].wait()
            for d in (1, 3, 2):
                first(h, c, d).wait_recv()
            for e in (1, 3, 2):
                second(h, c, e).start()
            keep(h, c).start()

    def weigh(d):
        n = shared(d)
        for q in range(n):
            sib(d, q).wait_recv()
        lanes = 2 * n * SHARD
        at_row = lax.broadcasted_iota(jnp.int32, (NOCC, lanes), 0)
        lane = lax.broadcasted_iota(jnp.int32, (NOCC, lanes), 1)
        q, j = lane // SHARD, lane % SHARD
        if n == 2:
            from_z = jnp.where(q % 2 == 0, z - d + DEPTH, z + d) % DEPTH
        else:
            from_z = (z + d) % DEPTH
        from_core = jnp.where(q < n, core, 1 - core)
        to = (from_z * 2 + from_core) * PANEL + j
        place = ((to == at_row) & (j < PANEL)).astype(jnp.float32).astype(jnp.bfloat16)
        parts = []
        for k in range(SLOTS):
            g = green[d][nbr[k, row], pl.ds(0, lanes), :]
            parts.append(jnp.where(k < cnt[row], g, jnp.zeros_like(g)))
        w32[...] += jnp.dot(
            place, jnp.concatenate(parts, axis=1), preferred_element_type=jnp.float32
        )

    def depart(q):
        for p in range(PARTS):
            ring(0, q, p).start()

    for c in range(CHUNKS):
        for d in (1, 3, 2):
            for h in range(2):
                first(h, c, d).start()
    sib(0, 0).start()

    @pl.when(up_first)
    def _():
        depart(0)

    @pl.when(down_first)
    def _():
        depart(1)

    @pl.when(jnp.logical_not(up_first))
    def _():
        pl.semaphore_wait(ready.at[1], 1)
        depart(0)

    @pl.when(jnp.logical_not(down_first))
    def _():
        pl.semaphore_wait(ready.at[0], 1)
        depart(1)

    for cp in tables:
        cp.wait()
    for d in range(1, FAR + 1):
        ring_step(d)
        if 3 <= d < 3 + CHUNKS:
            forward(d - 3)
        weigh(d - 1)
    weigh(FAR)
    w16[...] = w32[...].astype(jnp.bfloat16)
    store = pltpu.make_async_copy(w16, wout, local.at[0])
    store.start()

    for h in range(2):
        for c in range(CHUNKS):
            keep(h, c).wait()
            for d in (1, 3, 2):
                first(h, c, d).wait_send()
                second(h, c, d).wait_send()
                second(h, c, d).wait_recv()
    for d in range(FAR):
        for q in range(2):
            for p in range(PARTS):
                if moves(d, q, p):
                    ring(d, q, p).wait_send()
    for d in range(FAR + 1):
        for q in range(shared(d)):
            sib(d, q).wait_send()
    store.wait()


def contract(blocks, weights, out):
    flat = [blocks[:, k].reshape(GROUP * BS, BS) for k in range(SLOTS)]
    res = lax.dot_general(
        weights[...], jnp.concatenate(flat, axis=1), (((1,), (1,)), ((), ())),
        preferred_element_type=jnp.float32,
    )
    for p in range(GROUP):
        out[p] = res[:, p * BS : (p + 1) * BS].astype(jnp.bfloat16)


def per_device(integrals, green_panel, neighbours, slot_counts):
    blocks = integrals.reshape(SIDE, SIDE, SLOTS, BS, BS)
    anywhere = pl.BlockSpec(memory_space=pl.ANY)
    bf16, f32 = jnp.bfloat16, jnp.float32
    dma = pltpu.SemaphoreType.DMA
    gathered, weights = pl.pallas_call(
        exchange,
        out_shape=[
            jax.ShapeDtypeStruct((SIDE, SIDE, SLOTS, BS, BS), bf16),
            jax.ShapeDtypeStruct((NOCC, WIDE), bf16),
        ],
        in_specs=[pl.BlockSpec(memory_space=pltpu.HBM)] * 4,
        out_specs=[anywhere, anywhere],
        scratch_shapes=[pltpu.VMEM((ATOMS, 4 * SHARD, BS), bf16)] * (FAR + 1)
        + [
            pltpu.SMEM((SLOTS, ATOMS), jnp.int32),
            pltpu.SMEM((ATOMS,), jnp.int32),
            pltpu.VMEM((PANEL, ATOMS * BS), bf16),
            pltpu.VMEM((2, CHUNKS, SIDE, SIDE, BS, BS), bf16),
            pltpu.VMEM((NOCC, WIDE), f32),
            pltpu.VMEM((NOCC, WIDE), bf16),
            pltpu.SemaphoreType.REGULAR((2,)),
            dma((FAR, 2, PARTS)),
            dma((FAR, 2, PARTS)),
            dma((FAR + 1, 2)),
            dma((FAR + 1, 2)),
            dma((2, CHUNKS, SIDE)),
            dma((2, CHUNKS, SIDE)),
            dma((2, CHUNKS, SIDE)),
            dma((2, CHUNKS, SIDE)),
            dma((3 + 4 * CHUNKS,)),
        ],
        compiler_params=pltpu.CompilerParams(
            collective_id=0, has_side_effects=True, vmem_limit_bytes=48 << 20
        ),
    )(blocks, green_panel, neighbours.T, slot_counts)
    result = pl.pallas_call(
        contract,
        grid=(ATOMS // GROUP,),
        out_shape=jax.ShapeDtypeStruct((ATOMS, NOCC, BS), bf16),
        in_specs=[
            pl.BlockSpec((GROUP, SLOTS, BS, BS), lambda g: (g, 0, 0, 0)),
            pl.BlockSpec((NOCC, WIDE), lambda g: (0, 0)),
        ],
        out_specs=pl.BlockSpec((GROUP, NOCC, BS), lambda g: (g, 0, 0)),
        compiler_params=pltpu.CompilerParams(vmem_limit_bytes=48 << 20),
    )(gathered.reshape(ATOMS, SLOTS, BS, BS), weights)
    return jnp.swapaxes(result, 1, 2)


def solution(mesh):
    return jax.shard_map(
        per_device,
        mesh=mesh,
        in_specs=(P(("col", "row"), None, None, None, None), P("col", None), P(), P()),
        out_specs=P("col", "row", None),
        check_vma=False,
    )
```

```python
import jax
import jax.numpy as jnp
from jax import lax
from jax.experimental import pallas as pl
from jax.experimental.pallas import tpu as pltpu
from jax.sharding import PartitionSpec as P

MESH = pl.DeviceIdType.MESH
SIDE = 4
DEPTH = 16
FAR = DEPTH // 2
ATOMS = 16
SLOTS = 6
BS = 128
PANEL = 15
SHARD = 16
PAIR = 2 * SHARD
NOCC = 480
WIDE = SLOTS * BS
PARTS = 2
NU = ATOMS // PARTS
HALF = SLOTS // 2
GROUP = 4
CHUNKS = HALF
NEXT = ((1, 0), (-1, 0), (1, 1), (-1, 1))
CHIPS = [(0, 0)] + [(q, d) for d in range(1, FAR + 1) for q in ((0, 1) if d < FAR else (0,))]
BATCH = 4
BATCHES = DEPTH // BATCH


def exchange(
    ints, panel, nbr_in, cnt_in, fin, weights,
    g0, g1, g2, g3,
    nbr, cnt, rows, mid, w32, w16,
    ready, ring_s, ring_r, sib_s, sib_r, one_s, one_r, two_s, two_r, local,
):
    batches = [g0, g1, g2, g3]
    row = lax.axis_index("row")
    col = lax.axis_index("col")
    x, y = row // SIDE, row % SIDE
    z, core = col // 2, col % 2

    def plane(dz):
        return (z + dz + DEPTH) % DEPTH

    def at(dx=0, dy=0, dz=0, dc=0):
        return (
            ((x + dx) % SIDE) * SIDE + (y + dy) % SIDE,
            plane(dz) * 2 + (core + dc) % 2,
        )

    earlier = [plane(o) < z for o, _ in NEXT]
    partners = [at(dx=d) for d in (1, 2, 3)] + [at(dy=d) for d in (1, 2, 3)] + [at(dc=1)]
    barrier = pltpu.get_barrier_semaphore()
    for p in partners:
        pl.semaphore_signal(barrier, inc=1, device_id=p, device_id_type=MESH)
    for i, (o, c) in enumerate(NEXT):

        @pl.when(jnp.logical_not(earlier[i]))
        def _():
            pl.semaphore_signal(barrier, inc=1, device_id=at(dz=o, dc=c), device_id_type=MESH)

    load = pltpu.make_async_copy(panel, rows, local.at[0])
    load.start()
    tables = [
        pltpu.make_async_copy(nbr_in, nbr, local.at[1]),
        pltpu.make_async_copy(cnt_in, cnt, local.at[2]),
    ]
    for cp in tables:
        cp.start()

    def source(h, c, d):
        if h == 0:
            return ints.at[(x + d) % SIDE, :, c]
        return ints.at[:, (y + d) % SIDE, HALF + c]

    def landing(h, c):
        return mid.at[h, c, x if h == 0 else y]

    own = []
    for c in range(CHUNKS):
        for h in range(2):
            cp = pltpu.make_async_copy(
                source(h, c, 0), landing(h, c), local.at[3 + h * CHUNKS + c]
            )
            cp.start()
            own.append(cp)
    load.wait()
    for nu in range(ATOMS):
        g0[nu, pl.ds(0, SHARD), :] = jnp.concatenate(
            [rows[:, nu * BS : (nu + 1) * BS], jnp.zeros((1, BS), jnp.bfloat16)], axis=0
        )
    w32[...] = jnp.zeros_like(w32)
    expected = len(partners)
    for e in earlier:
        expected = expected + e.astype(jnp.int32)
    pl.semaphore_wait(barrier, expected)
    for i, (o, c) in enumerate(NEXT):

        @pl.when(earlier[i])
        def _():
            pl.semaphore_signal(
                ready.at[i ^ 1], inc=1, device_id=at(dz=o, dc=c), device_id_type=MESH
            )

    def shard(q, d, mine, nus):
        n = CHIPS.index((q if 0 < d < FAR else 0, d))
        first = (n % BATCH) * PAIR + (0 if mine else SHARD)
        return batches[n // BATCH].at[nus, pl.ds(first, SHARD), :]

    def ring(q, d, p):
        nus = pl.ds(p * NU, NU)
        return pltpu.make_async_remote_copy(
            src_ref=shard(q, d - 1, True, nus),
            dst_ref=shard(q, d, True, nus),
            send_sem=ring_s.at[d, q, p],
            recv_sem=ring_r.at[d, q, p],
            device_id=at(dz=1 if q == 0 else -1),
            device_id_type=MESH,
        )

    def cross(q):
        nus = pl.ds(q * NU, NU)
        return pltpu.make_async_remote_copy(
            src_ref=shard(q, FAR - 1, True, nus),
            dst_ref=shard(q, FAR, False, nus),
            send_sem=ring_s.at[0, q, 0],
            recv_sem=ring_r.at[0, q, 0],
            device_id=at(dz=1 if q == 0 else -1, dc=1),
            device_id_type=MESH,
        )

    def moves(q, d, p):
        return d < FAR or q == p

    def sib(q, d):
        return pltpu.make_async_remote_copy(
            src_ref=shard(q, d, True, pl.ds(0, ATOMS)),
            dst_ref=shard(q, d, False, pl.ds(0, ATOMS)),
            send_sem=sib_s.at[d, q],
            recv_sem=sib_r.at[d, q],
            device_id=at(dc=1),
            device_id_type=MESH,
        )

    def first(h, c, d):
        return pltpu.make_async_remote_copy(
            src_ref=source(h, c, d),
            dst_ref=landing(h, c),
            send_sem=one_s.at[h, c, d],
            recv_sem=one_r.at[h, c, d],
            device_id=at(dx=d) if h == 0 else at(dy=d),
            device_id_type=MESH,
        )

    def held(h, c, e):
        return mid.at[h, c, :, (y + e) % SIDE if h == 0 else (x + e) % SIDE]

    def final(h, c):
        return fin.at[:, y, c] if h == 0 else fin.at[x, :, HALF + c]

    def second(h, c, e):
        return pltpu.make_async_remote_copy(
            src_ref=held(h, c, e),
            dst_ref=final(h, c),
            send_sem=two_s.at[h, c, e],
            recv_sem=two_r.at[h, c, e],
            device_id=at(dy=e) if h == 0 else at(dx=e),
            device_id_type=MESH,
        )

    def keep(h, c):
        return pltpu.make_async_copy(
            held(h, c, 0), final(h, c), local.at[3 + (2 + h) * CHUNKS + c]
        )

    def step(d):
        for p in range(PARTS):
            for q in range(2):
                if moves(q, d, p):
                    ring(q, d, p).wait_recv()
                    if d < FAR and moves(q, d + 1, p):
                        ring(q, d + 1, p).start()
                        if d + 1 == FAR:
                            cross(q).start()
        for q in range(2):
            if d < FAR:
                sib(q, d).start()
            else:
                cross(q).wait_recv()

    def forward(c):
        for h in range(2):
            own[c * 2 + h].wait()
            for d in (1, 3, 2):
                first(h, c, d).wait_recv()
            for e in (1, 3, 2):
                second(h, c, e).start()
            keep(h, c).start()

    def weigh(b):
        chips = CHIPS[b * BATCH : (b + 1) * BATCH]
        for q, d in chips:
            if d < FAR:
                sib(q, d).wait_recv()
        at_row = lax.broadcasted_iota(jnp.int32, (NOCC, BATCH * PAIR), 0)
        lane = lax.broadcasted_iota(jnp.int32, (1, BATCH * PAIR), 1)
        chip, within = lane // PAIR, lane % PAIR
        from_z = jnp.zeros_like(lane)
        for n, (q, d) in enumerate(chips):
            from_z = jnp.where(chip == n, plane(-d if q == 0 else d), from_z)
        from_core = jnp.where(within < SHARD, core, 1 - core)
        j = within % SHARD
        to_row = jnp.where(j < PANEL, (from_z * 2 + from_core) * PANEL + j, -1)
        place = (to_row == at_row).astype(jnp.float32).astype(jnp.bfloat16)
        parts = []
        for k in range(SLOTS):
            g = batches[b][nbr[k, row]]
            parts.append(jnp.where(k < cnt[row], g, jnp.zeros_like(g)))
        total = w32[...] + jnp.dot(
            place, jnp.concatenate(parts, axis=1), preferred_element_type=jnp.float32
        )
        if b + 1 < BATCHES:
            w32[...] = total
        else:
            w16[...] = total.astype(jnp.bfloat16)

    def depart(i):
        for p in range(PARTS):
            ring(i, 1, p).start()

    for c in range(CHUNKS):
        for d in (1, 3, 2):
            for h in range(2):
                first(h, c, d).start()
    sib(0, 0).start()
    for i in range(2):

        @pl.when(earlier[i])
        def _():
            depart(i)

    def depart_later(i):
        @pl.when(jnp.logical_not(earlier[i]))
        def _():
            pl.semaphore_wait(ready.at[i], 1)
            depart(i)

    depart_later(0)
    depart_later(1)
    for cp in tables:
        cp.wait()
    step(1)
    step(2)
    step(3)
    forward(0)
    step(4)
    forward(1)
    weigh(0)
    step(5)
    forward(2)
    weigh(1)
    step(6)
    for i in (2, 3):

        @pl.when(jnp.logical_not(earlier[i]))
        def _():
            pl.semaphore_wait(ready.at[i], 1)

    step(7)
    weigh(2)
    step(8)
    weigh(3)
    save = pltpu.make_async_copy(w16, weights, local.at[0])
    save.start()

    for h in range(2):
        for c in range(CHUNKS):
            keep(h, c).wait()
            for d in (1, 3, 2):
                first(h, c, d).wait_send()
                second(h, c, d).wait_send()
                second(h, c, d).wait_recv()
    for d in range(1, FAR + 1):
        for q in range(2):
            for p in range(PARTS):
                if moves(q, d, p):
                    ring(q, d, p).wait_send()
    for q, d in CHIPS:
        if d < FAR:
            sib(q, d).wait_send()
        else:
            cross(0).wait_send()
            cross(1).wait_send()
    save.wait()


def contract(blocks, weights, out, fin, w, obuf, sems):
    def fetch(g):
        group = pl.ds(g * GROUP, GROUP)
        return pltpu.make_async_copy(blocks.at[group], fin.at[group], sems.at[g])

    def store(g):
        group = pl.ds(g * GROUP, GROUP)
        return pltpu.make_async_copy(obuf.at[group], out.at[group], sems.at[groups + g])

    groups = ATOMS // GROUP
    load = pltpu.make_async_copy(weights, w, sems.at[2 * groups])
    load.start()
    for g in range(groups):
        fetch(g).start()
    load.wait()
    for g in range(groups):
        fetch(g).wait()
        rhs = [
            fin[g * GROUP : (g + 1) * GROUP, k].reshape(GROUP * BS, BS) for k in range(SLOTS)
        ]
        res = lax.dot_general(
            w[...], jnp.concatenate(rhs, axis=1), (((1,), (1,)), ((), ())),
            preferred_element_type=jnp.float32,
        )
        for p in range(GROUP):
            obuf[g * GROUP + p] = res[:, p * BS : (p + 1) * BS].astype(jnp.bfloat16)
        store(g).start()
    for g in range(groups):
        store(g).wait()


def per_device(integrals, green_panel, neighbours, slot_counts):
    blocks = integrals.reshape(SIDE, SIDE, SLOTS, BS, BS)
    anywhere = pl.BlockSpec(memory_space=pl.ANY)
    bf16, f32 = jnp.bfloat16, jnp.float32
    dma = pltpu.SemaphoreType.DMA
    gathered, weights = pl.pallas_call(
        exchange,
        out_shape=[
            jax.ShapeDtypeStruct((SIDE, SIDE, SLOTS, BS, BS), bf16),
            jax.ShapeDtypeStruct((NOCC, WIDE), bf16),
        ],
        in_specs=[anywhere] * 4,
        out_specs=[anywhere] * 2,
        scratch_shapes=[pltpu.VMEM((ATOMS, BATCH * PAIR, BS), bf16)] * BATCHES
        + [
            pltpu.SMEM((SLOTS, ATOMS), jnp.int32),
            pltpu.SMEM((ATOMS,), jnp.int32),
            pltpu.VMEM((PANEL, ATOMS * BS), bf16),
            pltpu.VMEM((2, CHUNKS, SIDE, SIDE, BS, BS), bf16),
            pltpu.VMEM((NOCC, WIDE), f32),
            pltpu.VMEM((NOCC, WIDE), bf16),
            pltpu.SemaphoreType.REGULAR((4,)),
            dma((FAR + 1, 2, PARTS)),
            dma((FAR + 1, 2, PARTS)),
            dma((FAR + 1, 2)),
            dma((FAR + 1, 2)),
            dma((2, CHUNKS, SIDE)),
            dma((2, CHUNKS, SIDE)),
            dma((2, CHUNKS, SIDE)),
            dma((2, CHUNKS, SIDE)),
            dma((3 + 4 * CHUNKS,)),
        ],
        compiler_params=pltpu.CompilerParams(
            collective_id=0, has_side_effects=True, vmem_limit_bytes=60 << 20
        ),
    )(blocks, green_panel, neighbours.T, slot_counts)
    result = pl.pallas_call(
        contract,
        out_shape=jax.ShapeDtypeStruct((ATOMS, NOCC, BS), bf16),
        in_specs=[anywhere] * 2,
        out_specs=anywhere,
        scratch_shapes=[
            pltpu.VMEM((ATOMS, SLOTS, BS, BS), bf16),
            pltpu.VMEM((NOCC, WIDE), bf16),
            pltpu.VMEM((ATOMS, NOCC, BS), bf16),
            dma((2 * ATOMS // GROUP + 1,)),
        ],
        compiler_params=pltpu.CompilerParams(vmem_limit_bytes=60 << 20),
    )(gathered.reshape(ATOMS, SLOTS, BS, BS), weights)
    return jnp.swapaxes(result, 1, 2)


def solution(mesh):
    return jax.shard_map(
        per_device,
        mesh=mesh,
        in_specs=(P(("col", "row"), None, None, None, None), P("col", None), P(), P()),
        out_specs=P("col", "row", None),
        check_vma=False,
    )
```

```python
import jax
import jax.numpy as jnp
from jax import lax
from jax.experimental import pallas as pl
from jax.experimental.pallas import tpu as pltpu
from jax.sharding import PartitionSpec as P

MESH = pl.DeviceIdType.MESH
SIDE = 4
DEPTH = 16
FAR = DEPTH // 2
ATOMS = 16
SLOTS = 6
BS = 128
PANEL = 15
SHARD = 16
PAIR = 2 * SHARD
NOCC = 480
WIDE = SLOTS * BS
PARTS = 2
NU = ATOMS // PARTS
HALF = SLOTS // 2
GROUP = 4
CHUNKS = HALF
NEXT = ((1, 0), (-1, 0), (1, 1), (-1, 1))
CHIPS = [(0, 0)] + [(q, d) for d in range(1, FAR + 1) for q in ((0, 1) if d < FAR else (0,))]
BATCH = 4
BATCHES = DEPTH // BATCH


def exchange(
    ints, panel, nbr_in, cnt_in, fin, weights, last_place, last_rows,
    g0, g1, g2, g3,
    nbr, cnt, rows, mid, w16, where_to, chosen,
    ready, ring_s, ring_r, sib_s, sib_r, one_s, one_r, two_s, two_r, local,
):
    batches = [g0, g1, g2, g3]
    row = lax.axis_index("row")
    col = lax.axis_index("col")
    x, y = row // SIDE, row % SIDE
    z, core = col // 2, col % 2

    def plane(dz):
        return (z + dz + DEPTH) % DEPTH

    def at(dx=0, dy=0, dz=0, dc=0):
        return (
            ((x + dx) % SIDE) * SIDE + (y + dy) % SIDE,
            plane(dz) * 2 + (core + dc) % 2,
        )

    earlier = [plane(o) < z for o, _ in NEXT]
    partners = [at(dx=d) for d in (1, 2, 3)] + [at(dy=d) for d in (1, 2, 3)] + [at(dc=1)]
    barrier = pltpu.get_barrier_semaphore()
    for p in partners:
        pl.semaphore_signal(barrier, inc=1, device_id=p, device_id_type=MESH)
    for i, (o, c) in enumerate(NEXT):

        @pl.when(jnp.logical_not(earlier[i]))
        def _():
            pl.semaphore_signal(barrier, inc=1, device_id=at(dz=o, dc=c), device_id_type=MESH)

    load = pltpu.make_async_copy(panel, rows, local.at[0])
    load.start()
    tables = [
        pltpu.make_async_copy(nbr_in, nbr, local.at[1]),
        pltpu.make_async_copy(cnt_in, cnt, local.at[2]),
    ]
    for cp in tables:
        cp.start()

    def source(h, c, d):
        if h == 0:
            return ints.at[(x + d) % SIDE, :, c]
        return ints.at[:, (y + d) % SIDE, HALF + c]

    def landing(h, c):
        return mid.at[h, c, x if h == 0 else y]

    own = []
    for c in range(CHUNKS):
        for h in range(2):
            cp = pltpu.make_async_copy(
                source(h, c, 0), landing(h, c), local.at[3 + h * CHUNKS + c]
            )
            cp.start()
            own.append(cp)
    load.wait()
    for nu in range(ATOMS):
        g0[nu, pl.ds(0, SHARD), :] = jnp.concatenate(
            [rows[:, nu * BS : (nu + 1) * BS], jnp.zeros((1, BS), jnp.bfloat16)], axis=0
        )
    expected = len(partners)
    for e in earlier:
        expected = expected + e.astype(jnp.int32)
    pl.semaphore_wait(barrier, expected)
    for i, (o, c) in enumerate(NEXT):

        @pl.when(earlier[i])
        def _():
            pl.semaphore_signal(
                ready.at[i ^ 1], inc=1, device_id=at(dz=o, dc=c), device_id_type=MESH
            )

    def shard(q, d, mine, nus):
        n = CHIPS.index((q if 0 < d < FAR else 0, d))
        first = (n % BATCH) * PAIR + (0 if mine else SHARD)
        return batches[n // BATCH].at[nus, pl.ds(first, SHARD), :]

    def ring(q, d, p):
        nus = pl.ds(p * NU, NU)
        return pltpu.make_async_remote_copy(
            src_ref=shard(q, d - 1, True, nus),
            dst_ref=shard(q, d, True, nus),
            send_sem=ring_s.at[d, q, p],
            recv_sem=ring_r.at[d, q, p],
            device_id=at(dz=1 if q == 0 else -1),
            device_id_type=MESH,
        )

    def cross(q):
        nus = pl.ds(q * NU, NU)
        return pltpu.make_async_remote_copy(
            src_ref=shard(q, FAR - 1, True, nus),
            dst_ref=shard(q, FAR, False, nus),
            send_sem=ring_s.at[0, q, 0],
            recv_sem=ring_r.at[0, q, 0],
            device_id=at(dz=1 if q == 0 else -1, dc=1),
            device_id_type=MESH,
        )

    def moves(q, d, p):
        return d < FAR or q == p

    def sib(q, d):
        return pltpu.make_async_remote_copy(
            src_ref=shard(q, d, True, pl.ds(0, ATOMS)),
            dst_ref=shard(q, d, False, pl.ds(0, ATOMS)),
            send_sem=sib_s.at[d, q],
            recv_sem=sib_r.at[d, q],
            device_id=at(dc=1),
            device_id_type=MESH,
        )

    def first(h, c, d):
        return pltpu.make_async_remote_copy(
            src_ref=source(h, c, d),
            dst_ref=landing(h, c),
            send_sem=one_s.at[h, c, d],
            recv_sem=one_r.at[h, c, d],
            device_id=at(dx=d) if h == 0 else at(dy=d),
            device_id_type=MESH,
        )

    def held(h, c, e):
        return mid.at[h, c, :, (y + e) % SIDE if h == 0 else (x + e) % SIDE]

    def final(h, c):
        return fin.at[:, y, c] if h == 0 else fin.at[x, :, HALF + c]

    def second(h, c, e):
        return pltpu.make_async_remote_copy(
            src_ref=held(h, c, e),
            dst_ref=final(h, c),
            send_sem=two_s.at[h, c, e],
            recv_sem=two_r.at[h, c, e],
            device_id=at(dy=e) if h == 0 else at(dx=e),
            device_id_type=MESH,
        )

    def keep(h, c):
        return pltpu.make_async_copy(
            held(h, c, 0), final(h, c), local.at[3 + (2 + h) * CHUNKS + c]
        )

    def step(d):
        for p in range(PARTS):
            for q in range(2):
                if moves(q, d, p):
                    ring(q, d, p).wait_recv()
                    if d < FAR and moves(q, d + 1, p):
                        ring(q, d + 1, p).start()
                        if d + 1 == FAR:
                            cross(q).start()
        for q in range(2):
            if d < FAR:
                sib(q, d).start()
            else:
                cross(q).wait_recv()

    def forward(c):
        for h in range(2):
            own[c * 2 + h].wait()
            for d in (1, 3, 2):
                first(h, c, d).wait_recv()
            for e in (1, 3, 2):
                second(h, c, e).start()
            keep(h, c).start()

    def place(b):
        at_row = lax.broadcasted_iota(jnp.int32, (NOCC, BATCH * PAIR), 0)
        lane = lax.broadcasted_iota(jnp.int32, (1, BATCH * PAIR), 1)
        chip, within = lane // PAIR, lane % PAIR
        from_z = jnp.zeros_like(lane)
        for n, (q, d) in enumerate(CHIPS[b * BATCH : (b + 1) * BATCH]):
            from_z = jnp.where(chip == n, plane(-d if q == 0 else d), from_z)
        from_core = jnp.where(within < SHARD, core, 1 - core)
        j = within % SHARD
        to_row = jnp.where(j < PANEL, (from_z * 2 + from_core) * PANEL + j, -1)
        return (to_row == at_row).astype(jnp.float32).astype(jnp.bfloat16)

    def choose(b):
        for q, d in CHIPS[b * BATCH : (b + 1) * BATCH]:
            if d < FAR:
                sib(q, d).wait_recv()
        parts = []
        for k in range(SLOTS):
            g = batches[b][nbr[k, row]]
            parts.append(jnp.where(k < cnt[row], g, jnp.zeros_like(g)))
        return jnp.concatenate(parts, axis=1)

    def weigh(b):
        part = jnp.dot(place(b), choose(b), preferred_element_type=jnp.float32)
        part = part.astype(jnp.bfloat16)
        if b == 0:
            w16[...] = part
        else:
            w16[...] += part

    def depart(i):
        for p in range(PARTS):
            ring(i, 1, p).start()

    for c in range(CHUNKS):
        for d in (1, 3, 2):
            for h in range(2):
                first(h, c, d).start()
    sib(0, 0).start()
    for i in range(2):

        @pl.when(earlier[i])
        def _():
            depart(i)

    def depart_later(i):
        @pl.when(jnp.logical_not(earlier[i]))
        def _():
            pl.semaphore_wait(ready.at[i], 1)
            depart(i)

    depart_later(0)
    depart_later(1)
    for cp in tables:
        cp.wait()
    where_to[...] = place(BATCHES - 1)
    save_place = pltpu.make_async_copy(where_to, last_place, local.at[2])
    save_place.start()
    step(1)
    step(2)
    step(3)
    forward(0)
    step(4)
    forward(1)
    weigh(0)
    step(5)
    forward(2)
    weigh(1)
    step(6)
    for i in (2, 3):

        @pl.when(jnp.logical_not(earlier[i]))
        def _():
            pl.semaphore_wait(ready.at[i], 1)

    step(7)
    weigh(2)
    save = pltpu.make_async_copy(w16, weights, local.at[0])
    save.start()
    step(8)
    chosen[...] = choose(BATCHES - 1)
    save_rows = pltpu.make_async_copy(chosen, last_rows, local.at[1])
    save_rows.start()
    for h in range(2):
        for c in range(CHUNKS):
            keep(h, c).wait()
            for d in (1, 3, 2):
                first(h, c, d).wait_send()
                second(h, c, d).wait_send()
                second(h, c, d).wait_recv()
    for d in range(1, FAR + 1):
        for q in range(2):
            for p in range(PARTS):
                if moves(q, d, p):
                    ring(q, d, p).wait_send()
    for q, d in CHIPS:
        if d < FAR:
            sib(q, d).wait_send()
        else:
            cross(0).wait_send()
            cross(1).wait_send()
    save.wait()
    save_place.wait()
    save_rows.wait()


def contract(
    blocks, weights, last_place, last_rows, out, fin, w, where_to, chosen, obuf, sems
):
    def fetch(g):
        group = pl.ds(g * GROUP, GROUP)
        return pltpu.make_async_copy(blocks.at[group], fin.at[group], sems.at[g])

    def store(g):
        group = pl.ds(g * GROUP, GROUP)
        return pltpu.make_async_copy(obuf.at[group], out.at[group], sems.at[groups + g])

    groups = ATOMS // GROUP
    loads = [
        pltpu.make_async_copy(weights, w, sems.at[2 * groups]),
        pltpu.make_async_copy(last_place, where_to, sems.at[2 * groups + 1]),
        pltpu.make_async_copy(last_rows, chosen, sems.at[2 * groups + 2]),
    ]
    for cp in loads:
        cp.start()
    for g in range(groups):
        fetch(g).start()
    for cp in loads:
        cp.wait()
    last = jnp.dot(where_to[...], chosen[...], preferred_element_type=jnp.float32)
    w[...] += last.astype(jnp.bfloat16)
    for g in range(groups):
        fetch(g).wait()
        rhs = [
            fin[g * GROUP : (g + 1) * GROUP, k].reshape(GROUP * BS, BS) for k in range(SLOTS)
        ]
        res = lax.dot_general(
            w[...], jnp.concatenate(rhs, axis=1), (((1,), (1,)), ((), ())),
            preferred_element_type=jnp.float32,
        )
        for p in range(GROUP):
            obuf[g * GROUP + p] = res[:, p * BS : (p + 1) * BS].astype(jnp.bfloat16)
        store(g).start()
    for g in range(groups):
        store(g).wait()


def per_device(integrals, green_panel, neighbours, slot_counts):
    blocks = integrals.reshape(SIDE, SIDE, SLOTS, BS, BS)
    anywhere = pl.BlockSpec(memory_space=pl.ANY)
    bf16 = jnp.bfloat16
    dma = pltpu.SemaphoreType.DMA
    gathered, weights, last_place, last_rows = pl.pallas_call(
        exchange,
        out_shape=[
            jax.ShapeDtypeStruct((SIDE, SIDE, SLOTS, BS, BS), bf16),
            jax.ShapeDtypeStruct((NOCC, WIDE), bf16),
            jax.ShapeDtypeStruct((NOCC, BATCH * PAIR), bf16),
            jax.ShapeDtypeStruct((BATCH * PAIR, WIDE), bf16),
        ],
        in_specs=[anywhere] * 4,
        out_specs=[anywhere] * 4,
        scratch_shapes=[pltpu.VMEM((ATOMS, BATCH * PAIR, BS), bf16)] * BATCHES
        + [
            pltpu.SMEM((SLOTS, ATOMS), jnp.int32),
            pltpu.SMEM((ATOMS,), jnp.int32),
            pltpu.VMEM((PANEL, ATOMS * BS), bf16),
            pltpu.VMEM((2, CHUNKS, SIDE, SIDE, BS, BS), bf16),
            pltpu.VMEM((NOCC, WIDE), bf16),
            pltpu.VMEM((NOCC, BATCH * PAIR), bf16),
            pltpu.VMEM((BATCH * PAIR, WIDE), bf16),
            pltpu.SemaphoreType.REGULAR((4,)),
            dma((FAR + 1, 2, PARTS)),
            dma((FAR + 1, 2, PARTS)),
            dma((FAR + 1, 2)),
            dma((FAR + 1, 2)),
            dma((2, CHUNKS, SIDE)),
            dma((2, CHUNKS, SIDE)),
            dma((2, CHUNKS, SIDE)),
            dma((2, CHUNKS, SIDE)),
            dma((3 + 4 * CHUNKS,)),
        ],
        compiler_params=pltpu.CompilerParams(
            collective_id=0, has_side_effects=True, vmem_limit_bytes=60 << 20
        ),
    )(blocks, green_panel, neighbours.T, slot_counts)
    result = pl.pallas_call(
        contract,
        out_shape=jax.ShapeDtypeStruct((ATOMS, NOCC, BS), bf16),
        in_specs=[anywhere] * 4,
        out_specs=anywhere,
        scratch_shapes=[
            pltpu.VMEM((ATOMS, SLOTS, BS, BS), bf16),
            pltpu.VMEM((NOCC, WIDE), bf16),
            pltpu.VMEM((NOCC, BATCH * PAIR), bf16),
            pltpu.VMEM((BATCH * PAIR, WIDE), bf16),
            pltpu.VMEM((ATOMS, NOCC, BS), bf16),
            dma((2 * ATOMS // GROUP + 3,)),
        ],
        compiler_params=pltpu.CompilerParams(vmem_limit_bytes=60 << 20),
    )(gathered.reshape(ATOMS, SLOTS, BS, BS), weights, last_place, last_rows)
    return jnp.swapaxes(result, 1, 2)


def solution(mesh):
    return jax.shard_map(
        per_device,
        mesh=mesh,
        in_specs=(P(("col", "row"), None, None, None, None), P("col", None), P(), P()),
        out_specs=P("col", "row", None),
        check_vma=False,
    )
```

```python
import jax
import jax.numpy as jnp
from jax import lax
from jax.experimental import pallas as pl
from jax.experimental.pallas import tpu as pltpu
from jax.sharding import PartitionSpec as P

MESH = pl.DeviceIdType.MESH
SIDE = 4
DEPTH = 16
FAR = DEPTH // 2
ATOMS = 16
SLOTS = 6
BS = 128
PANEL = 15
SHARD = 16
PAIR = 2 * SHARD
NOCC = 480
WIDE = SLOTS * BS
PARTS = 2
NU = ATOMS // PARTS
HALF = SLOTS // 2
GROUP = 4
CHUNKS = HALF
NEXT = ((1, 0), (-1, 0), (1, 1), (-1, 1))
CHIPS = [(0, 0)] + [(q, d) for d in range(1, FAR + 1) for q in ((0, 1) if d < FAR else (0,))]
BATCH = 4
BATCHES = DEPTH // BATCH


def exchange(
    ints, panel, nbr_in, cnt_in, fin, weights, last_place, last_rows,
    g0, g1, g2, g3,
    nbr, cnt, rows, mid, w16, where_to, chosen,
    ready, ring_s, ring_r, sib_s, sib_r, one_s, one_r, two_s, two_r, local,
):
    batches = [g0, g1, g2, g3]
    row = lax.axis_index("row")
    col = lax.axis_index("col")
    x, y = row // SIDE, row % SIDE
    z, core = col // 2, col % 2

    def plane(dz):
        return (z + dz + DEPTH) % DEPTH

    def at(dx=0, dy=0, dz=0, dc=0):
        return (
            ((x + dx) % SIDE) * SIDE + (y + dy) % SIDE,
            plane(dz) * 2 + (core + dc) % 2,
        )

    earlier = [plane(o) < z for o, _ in NEXT]
    partners = [at(dx=d) for d in (1, 2, 3)] + [at(dy=d) for d in (1, 2, 3)] + [at(dc=1)]
    barrier = pltpu.get_barrier_semaphore()
    for p in partners:
        pl.semaphore_signal(barrier, inc=1, device_id=p, device_id_type=MESH)
    for i, (o, c) in enumerate(NEXT):

        @pl.when(jnp.logical_not(earlier[i]))
        def _():
            pl.semaphore_signal(barrier, inc=1, device_id=at(dz=o, dc=c), device_id_type=MESH)

    load = pltpu.make_async_copy(panel, rows, local.at[0])
    load.start()
    tables = [
        pltpu.make_async_copy(nbr_in, nbr, local.at[1]),
        pltpu.make_async_copy(cnt_in, cnt, local.at[2]),
    ]
    for cp in tables:
        cp.start()

    def source(h, c, d):
        if h == 0:
            return ints.at[(x + d) % SIDE, :, c]
        return ints.at[:, (y + d) % SIDE, HALF + c]

    def landing(h, c):
        return mid.at[h, c, x if h == 0 else y]

    own = []
    for c in range(CHUNKS):
        for h in range(2):
            cp = pltpu.make_async_copy(
                source(h, c, 0), landing(h, c), local.at[3 + h * CHUNKS + c]
            )
            cp.start()
            own.append(cp)
    load.wait()
    for nu in range(ATOMS):
        g0[nu, pl.ds(0, SHARD), :] = jnp.concatenate(
            [rows[:, nu * BS : (nu + 1) * BS], jnp.zeros((1, BS), jnp.bfloat16)], axis=0
        )
    expected = len(partners)
    for e in earlier:
        expected = expected + e.astype(jnp.int32)
    pl.semaphore_wait(barrier, expected)
    for i, (o, c) in enumerate(NEXT):

        @pl.when(earlier[i])
        def _():
            pl.semaphore_signal(
                ready.at[i ^ 1], inc=1, device_id=at(dz=o, dc=c), device_id_type=MESH
            )

    def shard(q, d, mine, nus):
        n = CHIPS.index((q if 0 < d < FAR else 0, d))
        first = (n % BATCH) * PAIR + (0 if mine else SHARD)
        return batches[n // BATCH].at[nus, pl.ds(first, SHARD), :]

    def ring(q, d, p):
        nus = pl.ds(p * NU, NU)
        return pltpu.make_async_remote_copy(
            src_ref=shard(q, d - 1, True, nus),
            dst_ref=shard(q, d, True, nus),
            send_sem=ring_s.at[d, q, p],
            recv_sem=ring_r.at[d, q, p],
            device_id=at(dz=1 if q == 0 else -1),
            device_id_type=MESH,
        )

    def cross(q):
        nus = pl.ds(q * NU, NU)
        return pltpu.make_async_remote_copy(
            src_ref=shard(q, FAR - 1, True, nus),
            dst_ref=shard(q, FAR, False, nus),
            send_sem=ring_s.at[0, q, 0],
            recv_sem=ring_r.at[0, q, 0],
            device_id=at(dz=1 if q == 0 else -1, dc=1),
            device_id_type=MESH,
        )

    def moves(q, d, p):
        return d < FAR or q == p

    def sib(q, d):
        return pltpu.make_async_remote_copy(
            src_ref=shard(q, d, True, pl.ds(0, ATOMS)),
            dst_ref=shard(q, d, False, pl.ds(0, ATOMS)),
            send_sem=sib_s.at[d, q],
            recv_sem=sib_r.at[d, q],
            device_id=at(dc=1),
            device_id_type=MESH,
        )

    def first(h, c, d):
        return pltpu.make_async_remote_copy(
            src_ref=source(h, c, d),
            dst_ref=landing(h, c),
            send_sem=one_s.at[h, c, d],
            recv_sem=one_r.at[h, c, d],
            device_id=at(dx=d) if h == 0 else at(dy=d),
            device_id_type=MESH,
        )

    def held(h, c, e):
        return mid.at[h, c, :, (y + e) % SIDE if h == 0 else (x + e) % SIDE]

    def final(h, c):
        return fin.at[:, y, c] if h == 0 else fin.at[x, :, HALF + c]

    def second(h, c, e):
        return pltpu.make_async_remote_copy(
            src_ref=held(h, c, e),
            dst_ref=final(h, c),
            send_sem=two_s.at[h, c, e],
            recv_sem=two_r.at[h, c, e],
            device_id=at(dy=e) if h == 0 else at(dx=e),
            device_id_type=MESH,
        )

    def keep(h, c):
        return pltpu.make_async_copy(
            held(h, c, 0), final(h, c), local.at[3 + (2 + h) * CHUNKS + c]
        )

    def step(d):
        for p in range(PARTS):
            for q in range(2):
                if moves(q, d, p):
                    ring(q, d, p).wait_recv()
                    if d < FAR and moves(q, d + 1, p):
                        ring(q, d + 1, p).start()
                        if d + 1 == FAR:
                            cross(q).start()
        for q in range(2):
            if d < FAR:
                sib(q, d).start()
            else:
                cross(q).wait_recv()

    def forward(c):
        for h in range(2):
            own[c * 2 + h].wait()
            for d in (1, 3, 2):
                first(h, c, d).wait_recv()
            for e in (1, 3, 2):
                second(h, c, e).start()
            keep(h, c).start()

    def place(b):
        at_row = lax.broadcasted_iota(jnp.int32, (NOCC, BATCH * PAIR), 0)
        lane = lax.broadcasted_iota(jnp.int32, (1, BATCH * PAIR), 1)
        chip, within = lane // PAIR, lane % PAIR
        from_z = jnp.zeros_like(lane)
        for n, (q, d) in enumerate(CHIPS[b * BATCH : (b + 1) * BATCH]):
            from_z = jnp.where(chip == n, plane(-d if q == 0 else d), from_z)
        from_core = jnp.where(within < SHARD, core, 1 - core)
        j = within % SHARD
        to_row = jnp.where(j < PANEL, (from_z * 2 + from_core) * PANEL + j, -1)
        return (to_row == at_row).astype(jnp.float32).astype(jnp.bfloat16)

    def choose(b):
        for q, d in CHIPS[b * BATCH : (b + 1) * BATCH]:
            if d < FAR:
                sib(q, d).wait_recv()
        parts = []
        for k in range(SLOTS):
            g = batches[b][nbr[k, row]]
            parts.append(jnp.where(k < cnt[row], g, jnp.zeros_like(g)))
        return jnp.concatenate(parts, axis=1)

    def weigh(b):
        part = jnp.dot(place(b), choose(b), preferred_element_type=jnp.float32)
        part = part.astype(jnp.bfloat16)
        if b == 0:
            w16[...] = part
        else:
            w16[...] += part

    def depart(i):
        for p in range(PARTS):
            ring(i, 1, p).start()

    for c in range(CHUNKS):
        for d in (1, 3, 2):
            for h in range(2):
                first(h, c, d).start()
    sib(0, 0).start()
    for i in range(2):

        @pl.when(earlier[i])
        def _():
            depart(i)

    def depart_later(i):
        @pl.when(jnp.logical_not(earlier[i]))
        def _():
            pl.semaphore_wait(ready.at[i], 1)
            depart(i)

    depart_later(0)
    depart_later(1)
    for cp in tables:
        cp.wait()
    where_to[...] = place(BATCHES - 1)
    save_place = pltpu.make_async_copy(where_to, last_place, local.at[2])
    save_place.start()
    step(1)
    step(2)
    step(3)
    forward(0)
    step(4)
    step(5)
    forward(1)
    step(6)
    forward(2)
    for i in (2, 3):

        @pl.when(jnp.logical_not(earlier[i]))
        def _():
            pl.semaphore_wait(ready.at[i], 1)

    step(7)
    weigh(0)
    weigh(1)
    weigh(2)
    save = pltpu.make_async_copy(w16, weights, local.at[0])
    save.start()
    step(8)
    chosen[...] = choose(BATCHES - 1)
    save_rows = pltpu.make_async_copy(chosen, last_rows, local.at[1])
    save_rows.start()
    for h in range(2):
        for c in range(CHUNKS):
            keep(h, c).wait()
            for d in (1, 3, 2):
                first(h, c, d).wait_send()
                second(h, c, d).wait_send()
                second(h, c, d).wait_recv()
    for d in range(1, FAR + 1):
        for q in range(2):
            for p in range(PARTS):
                if moves(q, d, p):
                    ring(q, d, p).wait_send()
    for q, d in CHIPS:
        if d < FAR:
            sib(q, d).wait_send()
        else:
            cross(0).wait_send()
            cross(1).wait_send()
    save.wait()
    save_place.wait()
    save_rows.wait()


def contract(
    blocks, weights, last_place, last_rows, out, fin, w, where_to, chosen, obuf, sems
):
    def fetch(g):
        group = pl.ds(g * GROUP, GROUP)
        return pltpu.make_async_copy(blocks.at[group], fin.at[group], sems.at[g])

    def store(g):
        group = pl.ds(g * GROUP, GROUP)
        return pltpu.make_async_copy(obuf.at[group], out.at[group], sems.at[groups + g])

    groups = ATOMS // GROUP
    loads = [
        pltpu.make_async_copy(weights, w, sems.at[2 * groups]),
        pltpu.make_async_copy(last_place, where_to, sems.at[2 * groups + 1]),
        pltpu.make_async_copy(last_rows, chosen, sems.at[2 * groups + 2]),
    ]
    for cp in loads:
        cp.start()
    for g in range(groups):
        fetch(g).start()
    for cp in loads:
        cp.wait()
    last = jnp.dot(where_to[...], chosen[...], preferred_element_type=jnp.float32)
    w[...] += last.astype(jnp.bfloat16)
    for g in range(groups):
        fetch(g).wait()
        rhs = [
            fin[g * GROUP : (g + 1) * GROUP, k].reshape(GROUP * BS, BS) for k in range(SLOTS)
        ]
        res = lax.dot_general(
            w[...], jnp.concatenate(rhs, axis=1), (((1,), (1,)), ((), ())),
            preferred_element_type=jnp.float32,
        )
        for p in range(GROUP):
            obuf[g * GROUP + p] = res[:, p * BS : (p + 1) * BS].astype(jnp.bfloat16)
        store(g).start()
    for g in range(groups):
        store(g).wait()


def per_device(integrals, green_panel, neighbours, slot_counts):
    blocks = integrals.reshape(SIDE, SIDE, SLOTS, BS, BS)
    anywhere = pl.BlockSpec(memory_space=pl.ANY)
    bf16 = jnp.bfloat16
    dma = pltpu.SemaphoreType.DMA
    gathered, weights, last_place, last_rows = pl.pallas_call(
        exchange,
        out_shape=[
            jax.ShapeDtypeStruct((SIDE, SIDE, SLOTS, BS, BS), bf16),
            jax.ShapeDtypeStruct((NOCC, WIDE), bf16),
            jax.ShapeDtypeStruct((NOCC, BATCH * PAIR), bf16),
            jax.ShapeDtypeStruct((BATCH * PAIR, WIDE), bf16),
        ],
        in_specs=[anywhere] * 4,
        out_specs=[anywhere] * 4,
        scratch_shapes=[pltpu.VMEM((ATOMS, BATCH * PAIR, BS), bf16)] * BATCHES
        + [
            pltpu.SMEM((SLOTS, ATOMS), jnp.int32),
            pltpu.SMEM((ATOMS,), jnp.int32),
            pltpu.VMEM((PANEL, ATOMS * BS), bf16),
            pltpu.VMEM((2, CHUNKS, SIDE, SIDE, BS, BS), bf16),
            pltpu.VMEM((NOCC, WIDE), bf16),
            pltpu.VMEM((NOCC, BATCH * PAIR), bf16),
            pltpu.VMEM((BATCH * PAIR, WIDE), bf16),
            pltpu.SemaphoreType.REGULAR((4,)),
            dma((FAR + 1, 2, PARTS)),
            dma((FAR + 1, 2, PARTS)),
            dma((FAR + 1, 2)),
            dma((FAR + 1, 2)),
            dma((2, CHUNKS, SIDE)),
            dma((2, CHUNKS, SIDE)),
            dma((2, CHUNKS, SIDE)),
            dma((2, CHUNKS, SIDE)),
            dma((3 + 4 * CHUNKS,)),
        ],
        compiler_params=pltpu.CompilerParams(
            collective_id=0, has_side_effects=True, vmem_limit_bytes=60 << 20
        ),
    )(blocks, green_panel, neighbours.T, slot_counts)
    result = pl.pallas_call(
        contract,
        out_shape=jax.ShapeDtypeStruct((ATOMS, NOCC, BS), bf16),
        in_specs=[anywhere] * 4,
        out_specs=anywhere,
        scratch_shapes=[
            pltpu.VMEM((ATOMS, SLOTS, BS, BS), bf16),
            pltpu.VMEM((NOCC, WIDE), bf16),
            pltpu.VMEM((NOCC, BATCH * PAIR), bf16),
            pltpu.VMEM((BATCH * PAIR, WIDE), bf16),
            pltpu.VMEM((ATOMS, NOCC, BS), bf16),
            dma((2 * ATOMS // GROUP + 3,)),
        ],
        compiler_params=pltpu.CompilerParams(vmem_limit_bytes=60 << 20),
    )(gathered.reshape(ATOMS, SLOTS, BS, BS), weights, last_place, last_rows)
    return jnp.swapaxes(result, 1, 2)


def solution(mesh):
    return jax.shard_map(
        per_device,
        mesh=mesh,
        in_specs=(P(("col", "row"), None, None, None, None), P("col", None), P(), P()),
        out_specs=P("col", "row", None),
        check_vma=False,
    )
```

```python
import jax
import jax.numpy as jnp
from jax import lax
from jax.experimental import pallas as pl
from jax.experimental.pallas import tpu as pltpu
from jax.sharding import PartitionSpec as P

MESH = pl.DeviceIdType.MESH
SIDE = 4
DEPTH = 16
FAR = DEPTH // 2
ATOMS = 16
SLOTS = 6
BS = 128
PANEL = 15
SHARD = 16
PAIR = 2 * SHARD
NOCC = 480
WIDE = SLOTS * BS
PARTS = 2
NU = ATOMS // PARTS
HALF = SLOTS // 2
GROUP = 4
CHUNKS = HALF
NEXT = ((1, 0), (-1, 0), (1, 1), (-1, 1))
CHIPS = [(0, 0)] + [(q, d) for d in range(1, FAR + 1) for q in ((0, 1) if d < FAR else (0,))]
BATCH = 4
BATCHES = DEPTH // BATCH


def exchange(
    ints, panel, nbr_in, cnt_in, fin, weights, last_place, last_rows,
    g0, g1, g2, g3,
    nbr, cnt, rows, mid, w16, where_to, chosen,
    ready, ring_s, ring_r, sib_s, sib_r, one_s, one_r, two_s, two_r, local,
):
    batches = [g0, g1, g2, g3]
    row = lax.axis_index("row")
    col = lax.axis_index("col")
    x, y = row // SIDE, row % SIDE
    z, core = col // 2, col % 2

    def plane(dz):
        return (z + dz + DEPTH) % DEPTH

    def at(dx=0, dy=0, dz=0, dc=0):
        return (
            ((x + dx) % SIDE) * SIDE + (y + dy) % SIDE,
            plane(dz) * 2 + (core + dc) % 2,
        )

    earlier = [plane(o) < z for o, _ in NEXT]
    partners = [at(dx=d) for d in (1, 2, 3)] + [at(dy=d) for d in (1, 2, 3)] + [at(dc=1)]
    barrier = pltpu.get_barrier_semaphore()
    for p in partners:
        pl.semaphore_signal(barrier, inc=1, device_id=p, device_id_type=MESH)
    for i, (o, c) in enumerate(NEXT):

        @pl.when(jnp.logical_not(earlier[i]))
        def _():
            pl.semaphore_signal(barrier, inc=1, device_id=at(dz=o, dc=c), device_id_type=MESH)

    load = pltpu.make_async_copy(panel, rows, local.at[0])
    load.start()
    tables = [
        pltpu.make_async_copy(nbr_in, nbr, local.at[1]),
        pltpu.make_async_copy(cnt_in, cnt, local.at[2]),
    ]
    for cp in tables:
        cp.start()

    def source(h, c, d):
        if h == 0:
            return ints.at[(x + d) % SIDE, :, c]
        return ints.at[:, (y + d) % SIDE, HALF + c]

    def landing(h, c):
        return mid.at[h, c, x if h == 0 else y]

    own = []
    for c in range(CHUNKS):
        for h in range(2):
            cp = pltpu.make_async_copy(
                source(h, c, 0), landing(h, c), local.at[3 + h * CHUNKS + c]
            )
            cp.start()
            own.append(cp)
    load.wait()
    for nu in range(ATOMS):
        g0[nu, pl.ds(0, SHARD), :] = jnp.concatenate(
            [rows[:, nu * BS : (nu + 1) * BS], jnp.zeros((1, BS), jnp.bfloat16)], axis=0
        )
    expected = len(partners)
    for e in earlier:
        expected = expected + e.astype(jnp.int32)
    pl.semaphore_wait(barrier, expected)
    for i, (o, c) in enumerate(NEXT):

        @pl.when(earlier[i])
        def _():
            pl.semaphore_signal(
                ready.at[i ^ 1], inc=1, device_id=at(dz=o, dc=c), device_id_type=MESH
            )

    def shard(q, d, mine, nus):
        n = CHIPS.index((q if 0 < d < FAR else 0, d))
        first = (n % BATCH) * PAIR + (0 if mine else SHARD)
        return batches[n // BATCH].at[nus, pl.ds(first, SHARD), :]

    def ring(q, d, p):
        nus = pl.ds(p * NU, NU)
        return pltpu.make_async_remote_copy(
            src_ref=shard(q, d - 1, True, nus),
            dst_ref=shard(q, d, True, nus),
            send_sem=ring_s.at[d, q, p],
            recv_sem=ring_r.at[d, q, p],
            device_id=at(dz=1 if q == 0 else -1),
            device_id_type=MESH,
        )

    def cross(q):
        nus = pl.ds(q * NU, NU)
        return pltpu.make_async_remote_copy(
            src_ref=shard(q, FAR - 1, True, nus),
            dst_ref=shard(q, FAR, False, nus),
            send_sem=ring_s.at[0, q, 0],
            recv_sem=ring_r.at[0, q, 0],
            device_id=at(dz=1 if q == 0 else -1, dc=1),
            device_id_type=MESH,
        )

    def moves(q, d, p):
        return d < FAR or q == p

    def sib(q, d):
        return pltpu.make_async_remote_copy(
            src_ref=shard(q, d, True, pl.ds(0, ATOMS)),
            dst_ref=shard(q, d, False, pl.ds(0, ATOMS)),
            send_sem=sib_s.at[d, q],
            recv_sem=sib_r.at[d, q],
            device_id=at(dc=1),
            device_id_type=MESH,
        )

    def first(h, c, d):
        return pltpu.make_async_remote_copy(
            src_ref=source(h, c, d),
            dst_ref=landing(h, c),
            send_sem=one_s.at[h, c, d],
            recv_sem=one_r.at[h, c, d],
            device_id=at(dx=d) if h == 0 else at(dy=d),
            device_id_type=MESH,
        )

    def held(h, c, e):
        return mid.at[h, c, :, (y + e) % SIDE if h == 0 else (x + e) % SIDE]

    def final(h, c):
        return fin.at[:, y, c] if h == 0 else fin.at[x, :, HALF + c]

    def second(h, c, e):
        return pltpu.make_async_remote_copy(
            src_ref=held(h, c, e),
            dst_ref=final(h, c),
            send_sem=two_s.at[h, c, e],
            recv_sem=two_r.at[h, c, e],
            device_id=at(dy=e) if h == 0 else at(dx=e),
            device_id_type=MESH,
        )

    def keep(h, c):
        return pltpu.make_async_copy(
            held(h, c, 0), final(h, c), local.at[3 + (2 + h) * CHUNKS + c]
        )

    def step(d):
        for p in range(PARTS):
            for q in range(2):
                if moves(q, d, p):
                    ring(q, d, p).wait_recv()
                    if d < FAR and moves(q, d + 1, p):
                        ring(q, d + 1, p).start()
                        if d + 1 == FAR:
                            cross(q).start()
        for q in range(2):
            if d < FAR:
                sib(q, d).start()
            else:
                cross(q).wait_recv()

    def forward(c):
        for h in range(2):
            own[c * 2 + h].wait()
            for d in (1, 3, 2):
                first(h, c, d).wait_recv()
            for e in (1, 3, 2):
                second(h, c, e).start()
            keep(h, c).start()

    def place(b):
        at_row = lax.broadcasted_iota(jnp.int32, (NOCC, BATCH * PAIR), 0)
        lane = lax.broadcasted_iota(jnp.int32, (1, BATCH * PAIR), 1)
        chip, within = lane // PAIR, lane % PAIR
        from_z = jnp.zeros_like(lane)
        for n, (q, d) in enumerate(CHIPS[b * BATCH : (b + 1) * BATCH]):
            from_z = jnp.where(chip == n, plane(-d if q == 0 else d), from_z)
        from_core = jnp.where(within < SHARD, core, 1 - core)
        j = within % SHARD
        to_row = jnp.where(j < PANEL, (from_z * 2 + from_core) * PANEL + j, -1)
        return (to_row == at_row).astype(jnp.float32).astype(jnp.bfloat16)

    def choose(b):
        for q, d in CHIPS[b * BATCH : (b + 1) * BATCH]:
            if d < FAR:
                sib(q, d).wait_recv()
        parts = []
        for k in range(SLOTS):
            g = batches[b][nbr[k, row]]
            parts.append(jnp.where(k < cnt[row], g, jnp.zeros_like(g)))
        return jnp.concatenate(parts, axis=1)

    def weigh(b):
        part = jnp.dot(place(b), choose(b), preferred_element_type=jnp.float32)
        part = part.astype(jnp.bfloat16)
        if b == 0:
            w16[...] = part
        else:
            w16[...] += part

    def depart(i):
        for p in range(PARTS):
            ring(i, 1, p).start()

    def set_out(c):
        for d in (1, 3, 2):
            for h in range(2):
                first(h, c, d).start()

    set_out(0)
    for i in range(2):

        @pl.when(earlier[i])
        def _():
            depart(i)

    for c in range(1, CHUNKS):
        set_out(c)
    sib(0, 0).start()

    def depart_later(i):
        @pl.when(jnp.logical_not(earlier[i]))
        def _():
            pl.semaphore_wait(ready.at[i], 1)
            depart(i)

    depart_later(0)
    depart_later(1)
    for cp in tables:
        cp.wait()
    where_to[...] = place(BATCHES - 1)
    save_place = pltpu.make_async_copy(where_to, last_place, local.at[2])
    save_place.start()
    step(1)
    step(2)
    step(3)
    forward(0)
    step(4)
    step(5)
    forward(1)
    step(6)
    forward(2)
    for i in (2, 3):

        @pl.when(jnp.logical_not(earlier[i]))
        def _():
            pl.semaphore_wait(ready.at[i], 1)

    step(7)
    weigh(0)
    weigh(1)
    weigh(2)
    save = pltpu.make_async_copy(w16, weights, local.at[0])
    save.start()
    step(8)
    chosen[...] = choose(BATCHES - 1)
    save_rows = pltpu.make_async_copy(chosen, last_rows, local.at[1])
    save_rows.start()
    for h in range(2):
        for c in range(CHUNKS):
            keep(h, c).wait()
            for d in (1, 3, 2):
                first(h, c, d).wait_send()
                second(h, c, d).wait_send()
                second(h, c, d).wait_recv()
    for d in range(1, FAR + 1):
        for q in range(2):
            for p in range(PARTS):
                if moves(q, d, p):
                    ring(q, d, p).wait_send()
    for q, d in CHIPS:
        if d < FAR:
            sib(q, d).wait_send()
        else:
            cross(0).wait_send()
            cross(1).wait_send()
    save.wait()
    save_place.wait()
    save_rows.wait()


def contract(
    blocks, weights, last_place, last_rows, out, fin, w, where_to, chosen, obuf, sems
):
    def fetch(g):
        group = pl.ds(g * GROUP, GROUP)
        return pltpu.make_async_copy(blocks.at[group], fin.at[group], sems.at[g])

    def store(g):
        group = pl.ds(g * GROUP, GROUP)
        return pltpu.make_async_copy(obuf.at[group], out.at[group], sems.at[groups + g])

    groups = ATOMS // GROUP
    loads = [
        pltpu.make_async_copy(weights, w, sems.at[2 * groups]),
        pltpu.make_async_copy(last_place, where_to, sems.at[2 * groups + 1]),
        pltpu.make_async_copy(last_rows, chosen, sems.at[2 * groups + 2]),
    ]
    for cp in loads:
        cp.start()
    for g in range(groups):
        fetch(g).start()
    for cp in loads:
        cp.wait()
    last = jnp.dot(where_to[...], chosen[...], preferred_element_type=jnp.float32)
    w[...] += last.astype(jnp.bfloat16)
    for g in range(groups):
        fetch(g).wait()
        rhs = [
            fin[g * GROUP : (g + 1) * GROUP, k].reshape(GROUP * BS, BS) for k in range(SLOTS)
        ]
        res = lax.dot_general(
            w[...], jnp.concatenate(rhs, axis=1), (((1,), (1,)), ((), ())),
            preferred_element_type=jnp.float32,
        )
        for p in range(GROUP):
            obuf[g * GROUP + p] = res[:, p * BS : (p + 1) * BS].astype(jnp.bfloat16)
        store(g).start()
    for g in range(groups):
        store(g).wait()


def per_device(integrals, green_panel, neighbours, slot_counts):
    blocks = integrals.reshape(SIDE, SIDE, SLOTS, BS, BS)
    anywhere = pl.BlockSpec(memory_space=pl.ANY)
    bf16 = jnp.bfloat16
    dma = pltpu.SemaphoreType.DMA
    gathered, weights, last_place, last_rows = pl.pallas_call(
        exchange,
        out_shape=[
            jax.ShapeDtypeStruct((SIDE, SIDE, SLOTS, BS, BS), bf16),
            jax.ShapeDtypeStruct((NOCC, WIDE), bf16),
            jax.ShapeDtypeStruct((NOCC, BATCH * PAIR), bf16),
            jax.ShapeDtypeStruct((BATCH * PAIR, WIDE), bf16),
        ],
        in_specs=[anywhere] * 4,
        out_specs=[anywhere] * 4,
        scratch_shapes=[pltpu.VMEM((ATOMS, BATCH * PAIR, BS), bf16)] * BATCHES
        + [
            pltpu.SMEM((SLOTS, ATOMS), jnp.int32),
            pltpu.SMEM((ATOMS,), jnp.int32),
            pltpu.VMEM((PANEL, ATOMS * BS), bf16),
            pltpu.VMEM((2, CHUNKS, SIDE, SIDE, BS, BS), bf16),
            pltpu.VMEM((NOCC, WIDE), bf16),
            pltpu.VMEM((NOCC, BATCH * PAIR), bf16),
            pltpu.VMEM((BATCH * PAIR, WIDE), bf16),
            pltpu.SemaphoreType.REGULAR((4,)),
            dma((FAR + 1, 2, PARTS)),
            dma((FAR + 1, 2, PARTS)),
            dma((FAR + 1, 2)),
            dma((FAR + 1, 2)),
            dma((2, CHUNKS, SIDE)),
            dma((2, CHUNKS, SIDE)),
            dma((2, CHUNKS, SIDE)),
            dma((2, CHUNKS, SIDE)),
            dma((3 + 4 * CHUNKS,)),
        ],
        compiler_params=pltpu.CompilerParams(
            collective_id=0, has_side_effects=True, vmem_limit_bytes=60 << 20
        ),
    )(blocks, green_panel, neighbours.T, slot_counts)
    result = pl.pallas_call(
        contract,
        out_shape=jax.ShapeDtypeStruct((ATOMS, NOCC, BS), bf16),
        in_specs=[anywhere] * 4,
        out_specs=anywhere,
        scratch_shapes=[
            pltpu.VMEM((ATOMS, SLOTS, BS, BS), bf16),
            pltpu.VMEM((NOCC, WIDE), bf16),
            pltpu.VMEM((NOCC, BATCH * PAIR), bf16),
            pltpu.VMEM((BATCH * PAIR, WIDE), bf16),
            pltpu.VMEM((ATOMS, NOCC, BS), bf16),
            dma((2 * ATOMS // GROUP + 3,)),
        ],
        compiler_params=pltpu.CompilerParams(vmem_limit_bytes=60 << 20),
    )(gathered.reshape(ATOMS, SLOTS, BS, BS), weights, last_place, last_rows)
    return jnp.swapaxes(result, 1, 2)


def solution(mesh):
    return jax.shard_map(
        per_device,
        mesh=mesh,
        in_specs=(P(("col", "row"), None, None, None, None), P("col", None), P(), P()),
        out_specs=P("col", "row", None),
        check_vma=False,
    )
```
